32 devices in a mesh: seq: 4 (over y, x), tok: 8 (over z, core).
Axes of the slice: x: 2, y: 2, z: 4, core: 2. Of those that a mesh axis runs over, the one named last changes fastest.
Arguments:
- hidden_in: bfloat16 [32, 1024, 768], P('seq', 'tok'), may hold values from -6 to 6
- out_grad: bfloat16 [32, 1024, 768], P('seq', 'tok'), may hold values from -6 to 6
- lengths: int32 [32], P('seq'), may hold values from 20 to 1024, as said below
- w_zx: float32 [768, 3072], P('seq', 'tok')
- m_zx: float32 [768, 3072], P('seq', 'tok'), may hold values from -40 to 40
- v_zx: float32 [768, 3072], P('seq', 'tok'), may hold values from 4 to 16
- w_bc: float32 [768, 304], P('seq', 'tok')
- m_bc: float32 [768, 304], P('seq', 'tok'), may hold values from -40 to 40
- v_bc: float32 [768, 304], P('seq', 'tok'), may hold values from 4 to 16
- w_out: float32 [1536, 768], P('seq', 'tok')
- m_out: float32 [1536, 768], P('seq', 'tok'), may hold values from -40 to 40
- v_out: float32 [1536, 768], P('seq', 'tok'), may hold values from 4 to 16
- conv_w: float32 [4, 1792], replicated, may hold values from -3 to 3
- m_conv: float32 [4, 1792], replicated, may hold values from -64 to 64
- v_conv: float32 [4, 1792], replicated, may hold values from 8 to 32
- vectors: float32 [4216], replicated
- m_vec: float32 [4216], replicated, may hold values from -64 to 64
- v_vec: float32 [4216], replicated, may hold values from 8 to 32
Outputs:
- hidden_out: bfloat16 [32, 1024, 768], P('seq', 'tok')
- hidden_grad: bfloat16 [32, 1024, 768], P('seq', 'tok')
- m_zx_new: float32 [768, 3072], P('seq', 'tok')
- v_zx_new: float32 [768, 3072], P('seq', 'tok')
- w_zx_new: float32 [768, 3072], P('seq', 'tok')
- m_bc_new: float32 [768, 304], P('seq', 'tok')
- v_bc_new: float32 [768, 304], P('seq', 'tok')
- w_bc_new: float32 [768, 304], P('seq', 'tok')
- m_out_new: float32 [1536, 768], P('seq', 'tok')
- v_out_new: float32 [1536, 768], P('seq', 'tok')
- w_out_new: float32 [1536, 768], P('seq', 'tok')
- m_conv_new: float32 [4, 1792], replicated
- v_conv_new: float32 [4, 1792], replicated
- conv_w_new: float32 [4, 1792], replicated
- m_vec_new: float32 [4216], replicated
- v_vec_new: float32 [4216], replicated
- vectors_new: float32 [4216], replicated
- norms: float32 [2, 8], replicated
The draws below stay inside these ranges and needn't reach their ends.
Inputs may be any that keep to these rules, and one draw needn't show every extreme that they name: `lengths`: each aligned group of 8 sequences holds at least one of length 1024.
All inputs are finite; a program needn't handle non-finite values.
Results may differ from the reference program's by a relative error of at most 0.0044.
The reference program's roundings to bfloat16 on the way count: a program that leaves them out, or rounds other values in their place, can miss the bound.
Values may be sent and summed in bfloat16 or wider, within the bound.
No kernel may reach another device: no remote copies, remote signals or barrier semaphores. Data moves between devices by JAX's collectives and lax.ppermute only.
A program may use at most 256 MiB of HBM per device.

```python
import math
import jax
import jax.numpy as jnp
from jax import lax

D = 768
E = 1536
H = 24
P_SIZE = 64
N = 64
Q = 128
K = 4
L = 1024
MIN_LEN = 20
STEP = 10
SEQ_GROUP = 8
SEQUENCES = 32


def rising_matrix(key, rows, cols, fan):
    base = jnp.clip(jax.random.normal(key, (rows, cols), jnp.float32), -4.0, 4.0)
    row_scale = 0.5 + jnp.arange(rows, dtype=jnp.float32) / rows
    col_scale = 0.5 + jnp.arange(cols, dtype=jnp.float32) / cols
    return base * row_scale[:, None] * col_scale[None, :] / math.sqrt(fan)


def draw_w_zx(key, part):
    key = jax.random.fold_in(key, 1)
    return rising_matrix(key, D, 2 * E, D)


def draw_w_bc(key, part):
    key = jax.random.fold_in(key, 2)
    return rising_matrix(key, D, 4 * N + 2 * H, D)


def draw_w_out(key, part):
    key = jax.random.fold_in(key, 3)
    return rising_matrix(key, E, D, E)


def draw_vectors(key, part):
    key = jax.random.fold_in(key, 4)
    keys = jax.random.split(key, 6)
    gain_in = 0.6 * 3.0 ** (jnp.arange(D, dtype=jnp.float32) / D) * jax.random.uniform(keys[0], (D,), jnp.float32, 0.8, 1.2)
    gain_out = 0.6 * 3.0 ** (jnp.arange(E, dtype=jnp.float32) / E) * jax.random.uniform(keys[1], (E,), jnp.float32, 0.8, 1.2)
    conv_bias = jax.random.uniform(keys[2], (E + 4 * N,), jnp.float32, -0.5, 0.5)
    step_size = jnp.exp(jax.random.uniform(keys[3], (2 * H,), jnp.float32, math.log(0.001), math.log(0.1)))
    delta_bias = step_size + jnp.log(-jnp.expm1(-step_size))
    decay_log = jnp.log(jax.random.uniform(keys[4], (2 * H,), jnp.float32, 1.0, 16.0))
    skip_gain = jax.random.uniform(keys[5], (H,), jnp.float32, 0.5, 1.5)
    return jnp.concatenate([gain_in, gain_out, conv_bias, delta_bias, decay_log, skip_gain])


def draw_lengths(key, part):
    key = jax.random.fold_in(key, 5)
    first_key, second_key = jax.random.split(key)
    drawn = jax.random.randint(first_key, (SEQUENCES,), MIN_LEN, L + 1)
    group_count = SEQUENCES // SEQ_GROUP
    picked = jax.random.randint(second_key, (group_count,), 0, SEQ_GROUP)
    slot_index = jnp.arange(SEQUENCES) % SEQ_GROUP
    owner = jnp.arange(SEQUENCES) // SEQ_GROUP
    full_one = slot_index == picked[owner]
    return jnp.where(full_one, L, drawn).astype(jnp.int32)


def steps_of(rng, dims, cuts, least, top_value):
    def one(position, parts):
        heights = jax.random.uniform(jax.random.fold_in(jax.random.fold_in(rng, 6), position), (parts,), jnp.float32, least / len(cuts), top_value / len(cuts))
        return jnp.repeat(jnp.exp(heights), dims[position] // parts).reshape((-1,) + (1,) * (len(dims) - position - 1))

    factor_of = one(*cuts[0])
    for cut in cuts[1:]:
        factor_of = factor_of * one(*cut)
    return factor_of


def gaussian(rng, dims, scale, limit, cuts=(), kind=jnp.bfloat16):
    factor_of = steps_of(rng, dims, cuts, -0.22, 0.18) if cuts else 1.0
    values = jax.random.normal(rng, dims, jnp.float32) * scale * factor_of
    return jnp.minimum(jnp.maximum(values, -limit), limit).astype(kind)


def setup_inputs(seed: int = 0) -> dict:
    key_list = jax.random.split(jax.random.key(seed), 19)
    hidden_in = gaussian(key_list[0], (SEQUENCES, L, D), 1.0, 6.0, ((0, 4), (1, 8)))
    out_grad = gaussian(key_list[1], (SEQUENCES, L, D), 1.0, 6.0, ((0, 4), (1, 8)))
    lengths = draw_lengths(jax.random.fold_in(key_list[18], 71), 0)
    w_zx = draw_w_zx(jax.random.fold_in(key_list[18], 71), 0)
    m_zx = gaussian(key_list[4], (D, 2 * E), (max(1, SEQUENCES * L // 660) ** 0.5), 40.0, ((0, 4), (1, 8)), jnp.float32)
    v_zx = jnp.clip(4.0 + 12.0 * jax.random.uniform(key_list[5], (D, 2 * E), jnp.float32) ** steps_of(key_list[5], (D, 2 * E), ((0, 4), (1, 8)), -0.2, 0.2), 4.0, 16.0)
    w_bc = draw_w_bc(jax.random.fold_in(key_list[18], 71), 0)
    m_bc = gaussian(key_list[7], (D, 4 * N + 2 * H), (max(1, SEQUENCES * L // 660) ** 0.5), 40.0, ((0, 4), (1, 8)), jnp.float32)
    v_bc = jnp.clip(4.0 + 12.0 * jax.random.uniform(key_list[8], (D, 4 * N + 2 * H), jnp.float32) ** steps_of(key_list[8], (D, 4 * N + 2 * H), ((0, 4), (1, 8)), -0.2, 0.2), 4.0, 16.0)
    w_out = draw_w_out(jax.random.fold_in(key_list[18], 71), 0)
    m_out = gaussian(key_list[10], (E, D), (max(1, SEQUENCES * L // 660) ** 0.5), 40.0, ((0, 4), (1, 8)), jnp.float32)
    v_out = jnp.clip(4.0 + 12.0 * jax.random.uniform(key_list[11], (E, D), jnp.float32) ** steps_of(key_list[11], (E, D), ((0, 4), (1, 8)), -0.2, 0.2), 4.0, 16.0)
    conv_w = gaussian(key_list[12], (K, E + 4 * N), K ** -0.5, 3.0, (), jnp.float32)
    m_conv = gaussian(key_list[13], (K, E + 4 * N), (max(1, SEQUENCES * L // 330) ** 0.5), 64.0, (), jnp.float32)
    v_conv = jnp.clip(jax.random.uniform(key_list[14], (K, E + 4 * N), jnp.float32, 8.0, 32.0), 8.0, 32.0)
    vectors = draw_vectors(jax.random.fold_in(key_list[18], 71), 0)
    m_vec = gaussian(key_list[16], (D + 2 * E + 4 * N + 5 * H,), (max(1, SEQUENCES * L // 330) ** 0.5), 64.0, (), jnp.float32)
    v_vec = jnp.clip(jax.random.uniform(key_list[17], (D + 2 * E + 4 * N + 5 * H,), jnp.float32, 8.0, 32.0), 8.0, 32.0)
    return dict(hidden_in=hidden_in, out_grad=out_grad, lengths=lengths, w_zx=w_zx, m_zx=m_zx, v_zx=v_zx, w_bc=w_bc, m_bc=m_bc, v_bc=v_bc, w_out=w_out, m_out=m_out, v_out=v_out, conv_w=conv_w, m_conv=m_conv, v_conv=v_conv, vectors=vectors, m_vec=m_vec, v_vec=v_vec)


NORM_EPS = 1e-05
UPDATE_EPS = 1e-06
ADAM_EPS = 1e-06
FIRST_DECAY = 0.9
SECOND_DECAY = 0.999
WEIGHT_DECAY = 0.01
LEARN_RATE = 0.3
HIGHEST = lax.Precision.HIGHEST

@jax.custom_vjp
def low(v):
    return lax.optimization_barrier(v.astype(jnp.bfloat16)).astype(jnp.float32)

@jax.custom_vjp
def low_back(v):
    return v

def low_keep(v):
    return (low(v), None)

def low_pass(kept, grad):
    return (grad,)

def back_keep(v):
    return (v, None)

def back_low(kept, grad):
    return (low(grad),)
low.defvjp(low_keep, low_pass)
low_back.defvjp(back_keep, back_low)

def rms_scale(values, gain):
    return values * lax.rsqrt(lax.optimization_barrier(jnp.mean(values * values, -1, keepdims=True)) + NORM_EPS) * gain

def gate_scale(values, gate_in, gain):
    gated = values * jax.nn.silu(gate_in)
    return gated * lax.rsqrt(lax.optimization_barrier(jnp.mean(gated * gated, -1, keepdims=True)) + NORM_EPS) * gain

def run_conv(padded, kernel, offset_vec):
    span_rows = padded.shape[1] - (K - 1)
    summed = offset_vec + kernel[0] * padded[:, 0:span_rows]
    for offset in range(1, K):
        summed = summed + kernel[offset] * padded[:, offset:offset + span_rows]
    return jax.nn.silu(summed)

def stretch_scan(inputs, rates, in_map, out_map):
    groups, length, head_count, head_width = inputs.shape
    blocks = length // Q

    def split_blocks(tensor):
        shaped = tensor.reshape((groups, blocks, Q) + tensor.shape[2:])
        return jnp.moveaxis(shaped, 1, 0)
    positions = jnp.arange(Q)
    strict_lower = (positions[:, None] > positions[None, :])[None, :, :, None]
    initial = jnp.zeros((groups, head_count, head_width, in_map.shape[-1]), jnp.float32)

    def advance(carry_state, pieces):
        block_in, block_rate, block_enter, block_leave = pieces
        running = jnp.cumsum(block_rate, axis=1)
        before = running - block_rate
        spread = before[:, :, None, :] - running[:, None, :, :]
        decays = jnp.exp(jnp.where(strict_lower, spread, -1e+30))
        scores = jnp.einsum('gin,gjn->gij', block_leave, block_enter, precision=HIGHEST)
        weights = scores[..., None] * decays
        within = jnp.einsum('gijh,gjhp->gihp', weights, block_in, precision=HIGHEST)
        carried = jnp.einsum('gin,ghpn->gihp', block_leave, carry_state, precision=HIGHEST) * jnp.exp(before)[..., None]
        last_sum = running[:, -1, :]
        to_end = jnp.exp(last_sum[:, None, :] - running)
        state_new = carry_state * jnp.exp(last_sum)[:, :, None, None] + jnp.einsum('gjhp,gjn->ghpn', block_in * to_end[..., None], block_enter, precision=HIGHEST)
        return (state_new, within + carried)
    pieces = (split_blocks(inputs), split_blocks(rates), split_blocks(in_map), split_blocks(out_map))
    _, outputs = lax.scan(jax.checkpoint(advance), initial, pieces)
    return jnp.moveaxis(outputs, 0, 1).reshape(groups, length, head_count, head_width)

def mixer(conv_out, delta_raw, ssm_params, keep_mask):
    delta_bias = ssm_params[:2 * H]
    decay_log = ssm_params[2 * H:4 * H]
    skip_gain = ssm_params[4 * H:]
    delta = jax.nn.softplus(delta_raw + delta_bias) * keep_mask[..., None]
    rates = -delta * jnp.exp(decay_log)
    groups, length = (conv_out.shape[0], conv_out.shape[1])
    values = conv_out[..., :E].reshape(groups, length, H, P_SIZE)
    in_fwd = conv_out[..., E:E + N]
    out_fwd = conv_out[..., E + N:E + 2 * N]
    in_back = conv_out[..., E + 2 * N:E + 3 * N]
    out_back = conv_out[..., E + 3 * N:]
    forward_part = stretch_scan(values * delta[..., :H, None], rates[..., :H], in_fwd, out_fwd)
    reverse_part = jnp.flip(stretch_scan(jnp.flip(values * delta[..., H:, None], 1), jnp.flip(rates[..., H:], 1), jnp.flip(in_back, 1), jnp.flip(out_back, 1)), 1)
    mixed = forward_part + reverse_part + skip_gain[:, None] * values
    return mixed.reshape(groups, length, E)

def layer_block(hidden, seq_lengths, proj_zx, proj_bc, proj_out, kernel, params):
    keep_mask = (jnp.arange(L)[None, :] < seq_lengths[:, None]).astype(jnp.float32)
    normed = low(rms_scale(hidden, params[:D]))
    zx_out = jnp.einsum('gld,de->gle', normed, proj_zx, precision=HIGHEST)
    bc_out = jnp.einsum('gld,de->gle', normed, proj_bc, precision=HIGHEST)
    gate_in = low_back(zx_out[..., :E])
    pre_conv = low(low_back(jnp.concatenate([zx_out[..., E:], bc_out[..., :4 * N]], -1)))
    delta_raw = low(low_back(bc_out[..., 4 * N:]))
    padded = jnp.pad(pre_conv, ((0, 0), (K - 1, 0), (0, 0)))
    conv_out = low(low_back(run_conv(padded, kernel, params[D + E:D + 2 * E + 4 * N])))
    mixed = low(low_back(mixer(conv_out, delta_raw, params[D + 2 * E + 4 * N:], keep_mask)))
    gated_norm = low(gate_scale(mixed, gate_in, params[D:D + E]))
    branch = low_back(jnp.einsum('gle,ed->gld', gated_norm, proj_out, precision=HIGHEST))
    return hidden + keep_mask[..., None] * branch

def forward(hidden, proj_zx, proj_bc, proj_out, kernel, params, lengths):
    proj_zx = low(proj_zx)
    proj_bc = low(proj_bc)
    proj_out = low(proj_out)
    seq_total = hidden.shape[0]
    block_size = 4 if seq_total % 4 == 0 else 1
    hidden_blocks = hidden.reshape((seq_total // block_size, block_size) + hidden.shape[1:])
    length_blocks = lengths.reshape(seq_total // block_size, block_size)

    def one_block(pieces):
        return layer_block(pieces[0], pieces[1], proj_zx, proj_bc, proj_out, kernel, params)
    outputs = lax.map(jax.checkpoint(one_block), (hidden_blocks, length_blocks))
    return outputs.reshape(hidden.shape)

def adam_step(param, grad, first, second):
    first_new = FIRST_DECAY * first + (1.0 - FIRST_DECAY) * grad
    second_new = SECOND_DECAY * second + (1.0 - SECOND_DECAY) * grad * grad
    corrected = first_new / (1.0 - FIRST_DECAY ** STEP)
    scaled = jnp.sqrt(second_new / (1.0 - SECOND_DECAY ** STEP))
    return (first_new, second_new, corrected / (scaled + ADAM_EPS) + WEIGHT_DECAY * param)

def segment_norms(param, direction):
    edges = (0, D, D + E, D + 2 * E + 4 * N, param.shape[0])
    weight_sq = jnp.stack([jnp.sum(param[edges[index]:edges[index + 1]] * param[edges[index]:edges[index + 1]]) for index in range(4)])
    update_sq = jnp.stack([jnp.sum(direction[edges[index]:edges[index + 1]] * direction[edges[index]:edges[index + 1]]) for index in range(4)])
    ratios = jnp.sqrt(weight_sq) / jnp.sqrt(update_sq + UPDATE_EPS)
    spread = jnp.concatenate([jnp.zeros((edges[index + 1] - edges[index],), param.dtype) + ratios[index] for index in range(4)])
    return (weight_sq, update_sq, spread)

def reference(hidden_in, out_grad, lengths, w_zx, m_zx, v_zx, w_bc, m_bc, v_bc, w_out, m_out, v_out, conv_w, m_conv, v_conv, vectors, m_vec, v_vec):

    def run(hidden, proj_zx, proj_bc, proj_out, kernel, params):
        return forward(hidden, proj_zx, proj_bc, proj_out, kernel, params, lengths)
    result, pullback = jax.vjp(run, hidden_in.astype(jnp.float32), w_zx, w_bc, w_out, conv_w, vectors)
    gradients = pullback(out_grad.astype(jnp.float32))
    hidden_grad = gradients[0].astype(jnp.bfloat16)
    matrices = ((w_zx, gradients[1], m_zx, v_zx), (w_bc, gradients[2], m_bc, v_bc), (w_out, gradients[3], m_out, v_out), (conv_w, gradients[4], m_conv, v_conv))
    updated = []
    weight_list = []
    update_list = []
    for param, grad, first, second in matrices:
        first_new, second_new, direction = adam_step(param, grad, first, second)
        weight_sq = jnp.sum(param * param)
        update_sq = jnp.sum(direction * direction)
        ratio = jnp.sqrt(weight_sq) / jnp.sqrt(update_sq + UPDATE_EPS)
        updated.extend([first_new, second_new, param - LEARN_RATE * ratio * direction])
        weight_list.append(weight_sq[None])
        update_list.append(update_sq[None])
    vec_first, vec_second, vec_dir = adam_step(vectors, gradients[5], m_vec, v_vec)
    seg_weight, seg_update, seg_ratio = segment_norms(vectors, vec_dir)
    vectors_new = vectors - LEARN_RATE * seg_ratio * vec_dir
    norms = jnp.stack([jnp.sqrt(jnp.concatenate(weight_list + [seg_weight])), jnp.sqrt(jnp.concatenate(update_list + [seg_update]))])
    return (result.astype(jnp.bfloat16), hidden_grad, updated[0], updated[1], updated[2], updated[3], updated[4], updated[5], updated[6], updated[7], updated[8], updated[9], updated[10], updated[11], vec_first, vec_second, vectors_new, norms)
```

```python
import numpy as np
import jax
import jax.numpy as jnp
from jax import lax
from jax.experimental import pallas as pl
from jax.experimental.pallas import tpu as pltpu
from jax.sharding import PartitionSpec as P

D = 768
E = 1536
H = 24
P_SIZE = 64
N = 64
Q = 128
K = 4
L = 1024
STEP = 10


NORM_EPS = 1e-05
UPDATE_EPS = 1e-06
ADAM_EPS = 1e-06
FIRST_DECAY = 0.9
SECOND_DECAY = 0.999
WEIGHT_DECAY = 0.01
LEARN_RATE = 0.3
HIGHEST = lax.Precision.HIGHEST


QB = 128
XW = E
MW = 4 * N
CW = XW + MW
PW = CW + 128
PAIRS = H // 2
HALO = 16
CHUNK = 256
F32 = jnp.float32
LOG2_E = 1.4426950408889634
BF16 = jnp.bfloat16
VMEM_BYTES = 58 * 1024 * 1024
GROUP = 256
GROUPS = XW // GROUP
GROUP_HEADS = GROUP // P_SIZE


def dot(a, b):
    return jnp.dot(a, b, preferred_element_type=F32)


def dot_nt(a, b):
    return lax.dot_general(a, b, (((1,), (1,)), ((), ())), preferred_element_type=F32)


def dot_tn(a, b):
    return lax.dot_general(a, b, (((0,), (0,)), ((), ())), preferred_element_type=F32)


def dot_exact(a, b):
    return jnp.dot(a, b, preferred_element_type=F32, precision=HIGHEST)


def iota(shape, dim):
    return lax.broadcasted_iota(jnp.int32, shape, dim)


def sigmoid(value):
    return 0.5 + 0.5 * jnp.tanh(0.5 * value)


def split(value):
    high = value.astype(BF16)
    return high, (value - high.astype(F32)).astype(BF16)


def doubled(value):
    return jnp.concatenate([value, value], 1)


def halves(pair):
    lane = iota(pair.shape, 1)
    zero = jnp.zeros_like(pair)
    return jnp.concatenate(
        [jnp.where(lane < P_SIZE, pair, zero), jnp.where(lane < P_SIZE, zero, pair)], 0
    )


def keep_tile(length, block):
    rows = block * QB + iota((QB, QB), 0)
    return jnp.where((rows < length) & (iota((QB, QB), 1) < 2 * H), 1.0, 0.0).astype(F32)


def edge_row(run):
    return jnp.where(iota((1, QB), 1) < H, run[QB - 1 : QB], run[0:1])


def two_parts(tile):
    return jnp.concatenate(split(tile), 1)


def lanes(group):
    return slice(group * GROUP, (group + 1) * GROUP)


def back_lanes(group):
    return slice(XW + group * GROUP, XW + (group + 1) * GROUP)


def decay_of(before, run_t, delta_t, lower, head):
    back = H + head
    ahead = before[:, head : head + 1] - run_t[head : head + 1]
    behind = before[:, back : back + 1] - run_t[back : back + 1]
    decay = jnp.exp2(jnp.minimum(jnp.minimum(ahead, behind), 0.0))
    step = jnp.where(lower, delta_t[head : head + 1], delta_t[back : back + 1])
    return decay, step


def spread_matrix():
    col = np.arange(2 * XW)[None]
    row = np.arange(2 * QB)[:, None]
    return jnp.asarray(row % QB == H * (col // XW) + col % XW // P_SIZE, BF16)


def block_scores(in_fwd, out_fwd, in_back, out_back):
    row = iota((QB, QB), 0)
    col = iota((QB, QB), 1)
    lower = row > col
    ahead = dot_nt(out_fwd, in_fwd)
    behind = dot_nt(out_back, in_back)
    return lower, jnp.where(lower, ahead, jnp.where(row < col, behind, 0.0))


def conv_pieces(ext, taps, bias):
    total = bias
    for tap in range(K):
        total = total + taps[tap : tap + 1] * ext[HALO - (K - 1) + tap : HALO - (K - 1) + tap + QB]
    return total


def split_maps(maps):
    return tuple(maps[:, N * index : N * (index + 1)] for index in range(4))


def scan_forward_kernel(
    place_ref, pre_ref, halo_ref, taps_ref, ssm_ref, skip_ref, spread_ref,
    conv_ref, mixed_ref, run_ref, delta_ref, ahead_ref, behind_ref, slope_ref,
    conv_all, behind_all, ahead_state, behind_state,
):
    blocks = pl.num_programs(0) // 2
    step = pl.program_id(0)

    @pl.when(step < blocks)
    def first_phase():
        block = blocks - 1 - step
        rows = pl.ds(pl.multiple_of(block * QB, QB), QB)
        kept = pl.ds(pl.multiple_of(block * 2 * N, 2 * N), 2 * N)

        @pl.when(step == 0)
        def start():
            behind_state[...] = jnp.zeros_like(behind_state)

        raw = pre_ref[:, CW:].astype(F32) + ssm_ref[0:1]
        delta = (jnp.maximum(raw, 0.0) + jnp.log1p(jnp.exp(-jnp.abs(raw)))) * keep_tile(place_ref[3], block)
        rates = -delta * ssm_ref[1:2]
        row = iota((QB, QB), 0)
        col = iota((QB, QB), 1)
        run = jnp.where(
            col < H,
            dot_exact((row >= col).astype(F32), rates),
            dot_exact((row <= col).astype(F32), rates),
        )
        run_ref[rows, :] = run
        delta_ref[rows, :] = delta
        edge = edge_row(run)
        scale = two_parts(delta * jnp.exp(edge - run))
        edge_exp = two_parts(jnp.broadcast_to(jnp.exp(edge), (8, QB)))

        def convolve(cols):
            halo = jnp.where(block > 0, halo_ref[:, cols].astype(F32), 0.0)
            ext = jnp.concatenate([halo, pre_ref[:, cols].astype(F32)], 0)
            total = conv_pieces(ext, taps_ref[:, cols], taps_ref[K : K + 1, cols])
            gate = sigmoid(total)
            value = (total * gate).astype(BF16)
            conv_ref[:, cols] = value
            conv_all[rows, cols] = value
            slope_ref[:, cols] = gate * (1.0 + total * (1.0 - gate))
            return value

        maps = convolve(slice(XW, CW))
        in_back = maps[:, 2 * N : 3 * N]
        in_back = jnp.concatenate([in_back, in_back], 0)
        for group in range(GROUPS):
            cols = lanes(group)
            wide_scale = dot(scale, spread_ref[:, back_lanes(group)])
            wide_edge = dot(edge_exp, spread_ref[:, back_lanes(group)])[0:1]
            state = behind_state[:, cols]
            low = jnp.concatenate(split(state), 0)
            behind_ref[:, cols] = low
            behind_all[kept, cols] = low
            pushed = jnp.concatenate(split(convolve(cols).astype(F32) * wide_scale), 0)
            behind_state[:, cols] = state * wide_edge + dot_tn(in_back, pushed)

    @pl.when(step >= blocks)
    def second_phase():
        block = step - blocks
        rows = pl.ds(pl.multiple_of(block * QB, QB), QB)
        kept = pl.ds(pl.multiple_of(block * 2 * N, 2 * N), 2 * N)

        @pl.when(step == blocks)
        def start():
            ahead_state[...] = jnp.zeros_like(ahead_state)

        in_fwd, out_fwd, in_back, out_back = split_maps(conv_all[rows, XW:])
        delta = delta_ref[rows, :]
        run = run_ref[rows, :]
        before = run + delta * ssm_ref[1:2]
        run_t = (run * LOG2_E).T
        before_two = before * LOG2_E
        delta_t = delta.T
        edge = edge_row(run)
        before_exp = two_parts(jnp.exp(before))
        scale = two_parts(delta * jnp.exp(edge - run))
        edge_exp = two_parts(jnp.broadcast_to(jnp.exp(edge), (8, QB)))
        lower, scores = block_scores(in_fwd, out_fwd, in_back, out_back)
        two_in = jnp.concatenate([in_fwd, in_fwd], 0)
        two_out_fwd = doubled(out_fwd)
        two_out_back = doubled(out_back)

        def products(group):
            cols = lanes(group)
            state = ahead_state[:, cols]
            low = jnp.concatenate(split(state), 0)
            ahead_ref[:, cols] = low
            return (
                state,
                dot(two_out_fwd, low),
                dot(two_out_back, behind_all[kept, cols]),
                dot(before_exp, spread_ref[:, cols]),
                dot(before_exp, spread_ref[:, back_lanes(group)]),
                dot(scale, spread_ref[:, cols]),
                dot(edge_exp, spread_ref[:, cols])[0:1],
            )

        ready = products(0)
        for group in range(GROUPS):
            state, carried_f, carried_b, wide_f, wide_b, wide_scale, wide_edge = ready
            if group + 1 < GROUPS:
                ready = products(group + 1)
            cols = lanes(group)
            values = conv_all[rows, cols]
            within = []
            for pair in range(2):
                weights = []
                for place in range(2):
                    head = group * GROUP_HEADS + 2 * pair + place
                    decay, size = decay_of(before_two, run_t, delta_t, lower, head)
                    weights.append(split(decay * scores * size))
                halved = halves(values[:, pair * QB : (pair + 1) * QB])
                weights = jnp.concatenate([weights[0][0], weights[1][0], weights[0][1], weights[1][1]], 1)
                within.append(dot(weights, jnp.concatenate([halved, halved], 0)))
            wide = values.astype(F32)
            mixed = jnp.concatenate(within, 1) + carried_f * wide_f + carried_b * wide_b
            mixed_ref[:, cols] = (mixed + wide * skip_ref[0:1, cols]).astype(BF16)
            pushed = jnp.concatenate(split(wide * wide_scale), 0)
            ahead_state[:, cols] = state * wide_edge + dot_tn(two_in, pushed)


def scan_backward_kernel(
    place_ref, grad_ref, conv_ref, pre_ref, slope_ref, run_ref, delta_ref, ahead_ref, behind_ref,
    taps_ref, ssm_ref, skip_ref, seg_ref, spread_ref,
    out_ref, other_ref, taps_grad_ref, ssm_grad_ref, skip_grad_ref,
    behind_grads, ahead_grad, behind_grad, col_rows, row_sums, next_rows,
):
    blocks = pl.num_programs(0) // 2
    step = pl.program_id(0)
    run = run_ref[...]
    delta = delta_ref[...]
    before = run + delta * ssm_ref[1:2]
    edge = edge_row(run)
    edge_exp = jnp.exp(edge)
    edge_parts = two_parts(jnp.broadcast_to(edge_exp, (8, QB)))
    before_exp = two_parts(jnp.exp(before))

    @pl.when(step < blocks)
    def first_phase():
        @pl.when(step == 0)
        def start():
            behind_grad[...] = jnp.zeros_like(behind_grad)

        kept = pl.ds(pl.multiple_of(step * 2 * N, 2 * N), 2 * N)
        out_back = conv_ref[:, XW + 3 * N : XW + 4 * N]
        for group in range(GROUPS):
            cols = lanes(group)
            state = behind_grad[:, cols]
            behind_grads[kept, cols] = jnp.concatenate(split(state), 0)
            wide = dot(before_exp, spread_ref[:, back_lanes(group)])
            wide_edge = dot(edge_parts, spread_ref[:, back_lanes(group)])[0:1]
            scaled = (grad_ref[:, cols].astype(F32) * wide).astype(BF16)
            behind_grad[:, cols] = state * wide_edge + dot_tn(out_back, scaled)

    @pl.when(step >= blocks)
    def second_phase():
        block = 2 * blocks - 1 - step
        kept = pl.ds(pl.multiple_of(block * 2 * N, 2 * N), 2 * N)

        @pl.when(step == blocks)
        def start():
            ahead_grad[...] = jnp.zeros_like(ahead_grad)
            taps_grad_ref[...] = jnp.zeros_like(taps_grad_ref)
            ssm_grad_ref[...] = jnp.zeros_like(ssm_grad_ref)
            skip_grad_ref[...] = jnp.zeros_like(skip_grad_ref)
            next_rows[...] = jnp.zeros_like(next_rows)
            col_rows[...] = jnp.zeros_like(col_rows)
            row_sums[...] = jnp.zeros_like(row_sums)

        lane = iota((QB, QB), 1)
        lane_row = iota((1, QB), 1)
        in_fwd, out_fwd, in_back, out_back = split_maps(conv_ref[:, XW:])
        run_t = (run * LOG2_E).T
        before_two = before * LOG2_E
        delta_t = delta.T
        to_edge = jnp.exp(edge - run)
        scale = delta * to_edge
        scale_parts = two_parts(scale)
        lower, scores = block_scores(in_fwd, out_fwd, in_back, out_back)
        two_out_fwd = doubled(out_fwd)
        two_out_back = doubled(out_back)
        two_in_fwd = doubled(in_fwd)
        two_in_back = doubled(in_back)

        def products(group):
            cols = lanes(group)
            state = ahead_grad[:, cols]
            ahead_low = jnp.concatenate(split(state), 0)
            behind_low = behind_grads[kept, cols]
            outer = [
                dot_nt(grad_ref[:, part], halves(conv_ref[:, part]))
                for part in (slice(base, base + QB) for base in range(cols.start, cols.stop, QB))
            ]
            return (
                outer,
                state,
                ahead_low[:N],
                behind_low[:N],
                dot(two_out_fwd, ahead_ref[:, cols]),
                dot(two_out_back, behind_ref[:, cols]),
                dot(two_in_fwd, ahead_low),
                dot(two_in_back, behind_low),
                dot(before_exp, spread_ref[:, cols]),
                dot(before_exp, spread_ref[:, back_lanes(group)]),
                dot(scale_parts, spread_ref[:, cols]),
                dot(scale_parts, spread_ref[:, back_lanes(group)]),
                dot(edge_parts, spread_ref[:, cols])[0:1],
            )

        def convolve(cols, value_grad):
            taps = taps_ref[:, cols]
            before_conv = pre_ref[:, cols].astype(F32)
            total_grad = value_grad.astype(F32) * slope_ref[:, cols]
            reach = jnp.concatenate([total_grad, next_rows[:, cols]], 0)
            taps_grad_ref[K : K + 1, cols] += jnp.sum(total_grad, 0, keepdims=True)
            result = jnp.zeros(before_conv.shape, F32)
            for tap in range(K):
                later = reach[K - 1 - tap : K - 1 - tap + QB]
                result = result + taps[tap : tap + 1] * later
                taps_grad_ref[tap : tap + 1, cols] += jnp.sum(before_conv * later, 0, keepdims=True)
            out_ref[:, cols] = result.astype(BF16)
            next_rows[:, cols] = total_grad[0:8]

        score_grad = jnp.zeros((QB, QB), F32)
        both_sums = jnp.zeros((2 * QB, QB), F32)
        out_fwd_grad = out_back_grad = in_fwd_grad = in_back_grad = jnp.zeros((QB, N), F32)
        held = jnp.zeros((1, QB), F32)
        ready = products(0)
        for group in range(GROUPS):
            (outer, state, ahead_low, behind_low, carried_f, carried_b, pulled_f, pulled_b,
             wide_f, wide_b, scale_f, scale_b, wide_edge) = ready
            if group + 1 < GROUPS:
                ready = products(group + 1)
            cols = lanes(group)
            values = conv_ref[:, cols]
            grads = grad_ref[:, cols]
            value_grad = []
            for pair in range(2):
                weights = []
                for place in range(2):
                    head = group * GROUP_HEADS + 2 * pair + place
                    decay, size = decay_of(before_two, run_t, delta_t, lower, head)
                    weights.append(split(decay * scores * size))
                    mixed = outer[pair][:, place * QB : (place + 1) * QB] * decay
                    score_grad = score_grad + mixed * size
                    direct = mixed * scores
                    direct_low = jnp.where(lower, direct, 0.0)
                    direct_sum = jnp.sum(direct, 0, keepdims=True)
                    direct_low_sum = jnp.sum(direct_low, 0, keepdims=True)
                    col_rows[head : head + 1, :] = direct_low_sum
                    col_rows[H + head : H + head + 1, :] = direct_sum - direct_low_sum
                    whole = direct * size
                    whole_sum = jnp.sum(whole, 1, keepdims=True)
                    whole_low_sum = jnp.sum(jnp.where(lower, whole, 0.0), 1, keepdims=True)
                    row_sums[:, head : head + 1] = whole_low_sum
                    row_sums[:, H + head : H + head + 1] = whole_sum - whole_low_sum
                halved = halves(grads[:, pair * QB : (pair + 1) * QB])
                weights = jnp.concatenate([weights[0][0], weights[1][0], weights[0][1], weights[1][1]], 0)
                value_grad.append(dot_tn(weights, jnp.concatenate([halved, halved], 0)))
            wide = values.astype(F32)
            wide_grad = grads.astype(F32)
            scaled_f = wide_grad * wide_f
            scaled_b = wide_grad * wide_b
            sums_f = jnp.concatenate([scaled_f * carried_f, wide * pulled_f], 0).astype(BF16)
            sums_b = jnp.concatenate([scaled_b * carried_b, wide * pulled_b], 0).astype(BF16)
            both_sums = both_sums + dot(sums_f, seg_ref[cols, :]) + dot(sums_b, seg_ref[back_lanes(group), :])
            scaled_f = scaled_f.astype(BF16)
            scaled_b = scaled_b.astype(BF16)
            ahead_in = ahead_ref[:N, cols]
            behind_in = behind_ref[:N, cols]
            out_fwd_grad = out_fwd_grad + dot_nt(scaled_f, ahead_in)
            out_back_grad = out_back_grad + dot_nt(scaled_b, behind_in)
            in_fwd_grad = in_fwd_grad + dot_nt((wide * scale_f).astype(BF16), ahead_low)
            in_back_grad = in_back_grad + dot_nt((wide * scale_b).astype(BF16), behind_low)
            result = jnp.concatenate(value_grad, 1) + scale_f * pulled_f + scale_b * pulled_b
            result = result + wide_grad * skip_ref[0:1, cols]
            ahead_grad[:, cols] = state * wide_edge + dot_tn(out_fwd, scaled_f)
            skip_grad_ref[0:1, cols] += jnp.sum(wide * wide_grad, 0, keepdims=True)
            for low, kept_state, shift in ((ahead_low, ahead_in, 0), (behind_low, behind_in, H)):
                product = jnp.sum(low.astype(F32) * kept_state.astype(F32), 0, keepdims=True)
                for pair in range(2):
                    part = product[:, pair * QB : (pair + 1) * QB]
                    for place in range(2):
                        inside = (lane_row < P_SIZE) if place == 0 else (lane_row >= P_SIZE)
                        total = jnp.sum(jnp.where(inside, part, 0.0), 1, keepdims=True)
                        held = jnp.where(lane_row == shift + group * GROUP_HEADS + 2 * pair + place, total, held)
            convolve(cols, result.astype(BF16))
        for part in split(jnp.where(iota((QB, QB), 0) > lane, score_grad, 0.0)):
            out_fwd_grad = out_fwd_grad + dot(part, in_fwd)
            in_fwd_grad = in_fwd_grad + dot_tn(part, out_fwd)
        for part in split(jnp.where(iota((QB, QB), 0) < lane, score_grad, 0.0)):
            out_back_grad = out_back_grad + dot(part, in_back)
            in_back_grad = in_back_grad + dot_tn(part, out_back)
        map_grads = jnp.concatenate([in_fwd_grad, out_fwd_grad, in_back_grad, out_back_grad], 1)
        convolve(slice(XW, CW), map_grads.astype(BF16))

        direct = col_rows[...].T
        column = delta * direct
        reached = both_sums[QB:]
        weighted = row_sums[...] + both_sums[:QB] - column
        entered = scale * reached
        first = jnp.where(lane < H, weighted, entered)
        second = jnp.where(lane < H, entered, weighted)
        row = iota((QB, QB), 0)
        rate_grad = dot_exact((row < lane).astype(F32), first) + dot_exact((row > lane).astype(F32), second)
        rate_grad = rate_grad - column + held * edge_exp
        delta_grad = direct + to_edge * reached - rate_grad * ssm_ref[1:2]
        raw = pre_ref[:, CW:].astype(F32) + ssm_ref[0:1]
        raw_grad = delta_grad * keep_tile(place_ref[3], block) * sigmoid(raw)
        ssm_grad_ref[0:1, :] += jnp.sum(raw_grad, 0, keepdims=True)
        ssm_grad_ref[1:2, :] += jnp.sum(rate_grad * (delta * -ssm_ref[1:2]), 0, keepdims=True)
        out_ref[:, CW:] = raw_grad.astype(BF16)
        for chip in range(2):
            col = pl.multiple_of((2 * chip + 1 - place_ref[2]) * TILE, QB)
            other_ref[:, chip * TILE : (chip + 1) * TILE] = out_ref[:, pl.ds(col, TILE)]
        other_ref[:, 2 * TILE :] = out_ref[:, XW:]

        @pl.when(block == 0)
        def finish():
            skip_heads = jnp.zeros((8, QB), F32)
            for part in split(jnp.broadcast_to(skip_grad_ref[0:1, :], (8, XW))):
                skip_heads = skip_heads + dot(part, seg_ref[:XW, :])
            ssm_grad_ref[2:3, :] = (
                ssm_grad_ref[0:1, :]
                + pltpu.roll(ssm_grad_ref[1:2, :], 2 * H, 1)
                + pltpu.roll(skip_heads[0:1], 4 * H, 1)
            )


def whole_spec(shape):
    return pl.BlockSpec(shape, lambda step: (0,) * len(shape))


def scan_forward(place, pre, taps, ssm, skip):
    total = pre.shape[0]
    blocks = total // QB

    def first(step):
        return jnp.maximum(blocks - 1 - step, 0)

    def second(step):
        return jnp.maximum(step - blocks, 0)

    per = QB // HALO
    return pl.pallas_call(
        scan_forward_kernel,
        grid=(2 * blocks,),
        in_specs=[
            pl.BlockSpec(memory_space=pltpu.SMEM),
            pl.BlockSpec((QB, PW), lambda step: (first(step), 0)),
            pl.BlockSpec((HALO, PW), lambda step: (jnp.maximum(first(step) * per - 1, 0), 0)),
            whole_spec((8, CW)),
            whole_spec((8, QB)),
            whole_spec((8, XW)),
            whole_spec((2 * QB, 2 * XW)),
        ],
        out_specs=[
            pl.BlockSpec((QB, CW), lambda step: (first(step), 0)),
            pl.BlockSpec((QB, XW), lambda step: (second(step), 0)),
            whole_spec((total, QB)),
            whole_spec((total, QB)),
            pl.BlockSpec((2 * N, XW), lambda step: (second(step), 0)),
            pl.BlockSpec((2 * N, XW), lambda step: (first(step), 0)),
            pl.BlockSpec((QB, CW), lambda step: (first(step), 0)),
        ],
        out_shape=[
            jax.ShapeDtypeStruct((total, CW), BF16),
            jax.ShapeDtypeStruct((total, XW), BF16),
            jax.ShapeDtypeStruct((total, QB), F32),
            jax.ShapeDtypeStruct((total, QB), F32),
            jax.ShapeDtypeStruct((2 * blocks * N, XW), BF16),
            jax.ShapeDtypeStruct((2 * blocks * N, XW), BF16),
            jax.ShapeDtypeStruct((total, CW), F32),
        ],
        scratch_shapes=[
            pltpu.VMEM((total, CW), BF16),
            pltpu.VMEM((2 * blocks * N, XW), BF16),
            pltpu.VMEM((N, XW), F32),
            pltpu.VMEM((N, XW), F32),
        ],
        compiler_params=pltpu.CompilerParams(vmem_limit_bytes=VMEM_BYTES),
        cost_estimate=pl.CostEstimate(flops=26000 * total * XW, bytes_accessed=1, transcendentals=0),
        name="scan_forward",
    )(place, pre, pre, taps, ssm, skip, spread_matrix())


def scan_backward(device, grads, conv_low, pre, slope, run, delta, ahead, behind, taps, ssm, skip):
    total = pre.shape[0]
    blocks = total // QB

    def place(step):
        return jnp.where(step < blocks, step, 2 * blocks - 1 - step)

    def late(step):
        return jnp.minimum(2 * blocks - 1 - step, blocks - 1)

    places = np.arange(2 * XW)[:, None]
    segment = np.arange(QB)[None] == H * (places // XW) + places % XW // P_SIZE
    segment = jnp.asarray(segment, BF16)
    row_block = lambda width, where: pl.BlockSpec((QB, width), lambda step: (where(step), 0))
    return pl.pallas_call(
        scan_backward_kernel,
        grid=(2 * blocks,),
        in_specs=[
            pl.BlockSpec(memory_space=pltpu.SMEM),
            row_block(XW, place),
            row_block(CW, place),
            row_block(PW, late),
            row_block(CW, late),
            row_block(QB, place),
            row_block(QB, place),
            pl.BlockSpec((2 * N, XW), lambda step: (late(step), 0)),
            pl.BlockSpec((2 * N, XW), lambda step: (late(step), 0)),
            whole_spec((8, CW)),
            whole_spec((8, QB)),
            whole_spec((8, XW)),
            whole_spec((2 * XW, QB)),
            whole_spec((2 * QB, 2 * XW)),
        ],
        out_specs=[
            row_block(PW, late),
            row_block(3 * TILE, late),
            whole_spec((8, CW)),
            whole_spec((8, QB)),
            whole_spec((8, XW)),
        ],
        out_shape=[
            jax.ShapeDtypeStruct((total, PW), BF16),
            jax.ShapeDtypeStruct((total, 3 * TILE), BF16),
            jax.ShapeDtypeStruct((8, CW), F32),
            jax.ShapeDtypeStruct((8, QB), F32),
            jax.ShapeDtypeStruct((8, XW), F32),
        ],
        scratch_shapes=[
            pltpu.VMEM((2 * blocks * N, XW), BF16),
            pltpu.VMEM((N, XW), F32),
            pltpu.VMEM((N, XW), F32),
            pltpu.VMEM((QB, QB), F32),
            pltpu.VMEM((QB, QB), F32),
            pltpu.VMEM((8, CW), F32),
        ],
        compiler_params=pltpu.CompilerParams(vmem_limit_bytes=VMEM_BYTES),
        cost_estimate=pl.CostEstimate(flops=48000 * total * XW, bytes_accessed=1, transcendentals=0),
        name="scan_backward",
    )(device, grads, conv_low, pre, slope, run, delta, ahead, behind, taps, ssm, skip, segment, spread_matrix())


TILE = 384
SEQS, CHIPS = 4, 4
ROWS_ZX, ROWS_OUT, ROWS_BC = D // SEQS, D // 8, 48
PIECE = 2 * ROWS_ZX + CHIPS // 2 * ROWS_BC
REST = 2 * ROWS_ZX + CHIPS * ROWS_OUT
BC_COLS = MW + 2 * H
BC_EACH = BC_COLS // 8
BC_LANES = 256
SMALL_EDGES = (0, K * CW, K * CW + D, K * CW + D + E, K * CW + D + E + CW, K * CW + D + E + CW + 5 * H)
SMALL_ROWS = 96
CONV_ROWS = K * CW // QB
CHUNK_ROW = 40
BLOCK = 256


def small_maps():
    inner = np.arange(8 * ROWS_BC)[None]
    std = np.arange(TILE)[:, None]
    row_map = (inner % ROWS_BC < BC_EACH) & (std == inner // ROWS_BC * BC_EACH + inner % ROWS_BC)
    inner = np.arange(SEQS * BC_LANES)[:, None]
    std = np.arange(D)[None]
    col_map = (inner % BC_LANES < ROWS_ZX) & (std == inner // BC_LANES * ROWS_ZX + inner % BC_LANES)
    return jnp.asarray(row_map, BF16), jnp.asarray(col_map, BF16)


def whole(shape):
    return pl.BlockSpec(shape, lambda *index: (0,) * len(shape))


def scalar_call(kernel, scalars, grid, inputs, in_specs, outs, out_specs, scratch=(), name=None, flops=1):
    spec = pltpu.PrefetchScalarGridSpec(
        num_scalar_prefetch=1, grid=grid, in_specs=in_specs, out_specs=out_specs, scratch_shapes=scratch
    )
    return pl.pallas_call(
        kernel,
        grid_spec=spec,
        out_shape=outs,
        compiler_params=pltpu.CompilerParams(vmem_limit_bytes=VMEM_BYTES),
        cost_estimate=pl.CostEstimate(flops=flops, bytes_accessed=1, transcendentals=0),
        name=name,
    )(scalars, *inputs)


def small_rows(chip):
    start = 2 * ROWS_ZX + chip // 2 * ROWS_BC
    return slice(start, start + ROWS_BC)


def half_row(value, chip):
    return pltpu.roll(value, ROWS_ZX, 1) if chip % 2 else value


def seq_rows(place, index, rows):
    return pl.ds(pl.multiple_of((place[0] ^ index) * rows, rows), rows)


def join_columns(place, refs, out_ref):
    for core in range(2):
        for index in range(SEQS):
            for chip in range(2):
                tile = 2 * ((place[1] & 1) ^ chip) + (place[2] ^ core)
                cols = pl.ds(pl.multiple_of(tile * TILE, QB), TILE)
                piece = refs[SEQS * core + index][chip * ROWS_ZX : (chip + 1) * ROWS_ZX, :]
                out_ref[seq_rows(place, index, ROWS_ZX), cols] = piece


def join_out(place, refs, out_ref):
    for index in range(SEQS):
        cols = pl.ds(pl.multiple_of((place[0] ^ index) * TILE, QB), TILE)
        for core in range(2):
            for chip in range(CHIPS):
                tok = 2 * (chip ^ place[1]) + (core ^ place[2])
                rows = pl.ds(pl.multiple_of(tok * ROWS_OUT, ROWS_OUT), ROWS_OUT)
                row = 2 * ROWS_ZX + chip * ROWS_OUT
                out_ref[rows, cols] = refs[SEQS * core + index][row : row + ROWS_OUT, :]


def join_weights(scalars, pieces):
    row_map, col_map = small_maps()

    def kernel(place, row_ref, col_ref, *refs):
        refs, (wide_ref, small_ref, small_pieces) = refs[: 2 * SEQS], refs[2 * SEQS :]
        join_columns(place, refs, wide_ref)
        for core in range(2):
            for index in range(SEQS):
                cols = pl.ds(pl.multiple_of((place[0] ^ index) * BC_LANES, BC_LANES), BC_LANES)
                for chip in range(CHIPS):
                    tok = 2 * (chip ^ place[1]) + (core ^ place[2])
                    rows = pl.ds(pl.multiple_of(tok * ROWS_BC, ROWS_BC), ROWS_BC)
                    piece = refs[SEQS * core + index][small_rows(chip), :].astype(F32)
                    small_pieces[rows, cols] = half_row(piece, chip)[:, :BC_LANES].astype(BF16)
        rows = dot(row_ref[...], small_pieces[...]).astype(BF16)
        small_ref[...] = dot(rows, col_ref[...]).astype(BF16)

    return scalar_call(
        kernel, scalars, (1,), (row_map, col_map, *pieces),
        [whole(row_map.shape), whole(col_map.shape)] + [whole((PIECE, TILE))] * (2 * SEQS),
        [jax.ShapeDtypeStruct((D, XW), BF16), jax.ShapeDtypeStruct((TILE, D), BF16)],
        [whole((D, XW)), whole((TILE, D))],
        scratch=[pltpu.VMEM((8 * ROWS_BC, SEQS * BC_LANES), BF16)],
        name="join_weights",
    )


def project(hidden, gain_in, inner_weights, small_weights):
    total = hidden.shape[0]

    def kernel(hidden_ref, gain_ref, wide_ref, small_ref, normed_ref, normed_t_ref, pre_ref):
        value = hidden_ref[...].astype(F32)
        scale = lax.rsqrt(jnp.mean(value * value, -1, keepdims=True) + NORM_EPS)
        normed = (value * scale * gain_ref[0:1]).astype(BF16)
        normed_ref[...] = normed
        normed_t_ref[...] = normed.T
        pre_ref[:, :XW] = dot(normed, wide_ref[...]).astype(BF16)
        pre_ref[:, XW:] = dot_nt(normed, small_ref[...]).astype(BF16)

    def rows(width):
        return pl.BlockSpec((BLOCK, width), lambda step: (step, 0))

    return pl.pallas_call(
        kernel,
        grid=(total // BLOCK,),
        in_specs=[rows(D), whole((8, D)), whole((D, XW)), whole((TILE, D))],
        out_specs=[rows(D), pl.BlockSpec((D, BLOCK), lambda step: (0, step)), rows(PW)],
        out_shape=[
            jax.ShapeDtypeStruct((total, D), BF16),
            jax.ShapeDtypeStruct((D, total), BF16),
            jax.ShapeDtypeStruct((total, PW), BF16),
        ],
        compiler_params=pltpu.CompilerParams(vmem_limit_bytes=VMEM_BYTES),
        cost_estimate=pl.CostEstimate(flops=8 * total * D * PW, bytes_accessed=1, transcendentals=0),
        name="project",
    )(hidden, gain_in, inner_weights, small_weights)


def gated_norm(scalars, normed, mixed, hidden, upstream, gain_out, pieces):
    total = hidden.shape[0]

    def kernel(place, normed_ref, mixed_ref, hidden_ref, upstream_ref, gain_ref, *refs):
        pieces, refs = refs[: 2 * SEQS], refs[2 * SEQS :]
        (hidden_out_ref, gated_ref, mixed_grad_ref, gate_grad_ref, branch_t_ref, gain_grad_ref, gate_w, out_w) = refs
        step = pl.program_id(0)

        @pl.when(step == 0)
        def start():
            gain_grad_ref[...] = jnp.zeros_like(gain_grad_ref)
            join_columns(place, pieces, gate_w)
            join_out(place, pieces, out_w)

        keep = jnp.where(step * BLOCK + iota((BLOCK, 1), 0) < place[3], 1.0, 0.0).astype(F32)
        gain = gain_ref[0:1]
        branch_grad = (upstream_ref[...].astype(F32) * keep).astype(BF16)
        branch_t_ref[...] = branch_grad.T
        gated_grad = dot(branch_grad, out_w[...])
        gate_in = dot(normed_ref[...], gate_w[...])
        sig = sigmoid(gate_in)
        gate = gate_in * sig
        mixed = mixed_ref[...].astype(F32)
        gated = mixed * gate
        scale = lax.rsqrt(jnp.mean(gated * gated, -1, keepdims=True) + NORM_EPS)
        unit = gated * scale
        gated_low = (unit * gain).astype(BF16)
        gated_ref[...] = gated_low
        branch = dot_nt(gated_low, out_w[...])
        hidden_out_ref[...] = (hidden_ref[...].astype(F32) + keep * branch).astype(BF16)
        gain_grad_ref[0:1] += jnp.sum(gated_grad * unit, 0, keepdims=True)
        pulled = gated_grad * gain
        inner = scale * (pulled - unit * jnp.mean(pulled * unit, -1, keepdims=True))
        mixed_grad_ref[...] = (inner * gate).astype(BF16)
        gate_grad_ref[...] = (inner * mixed * (sig * (1.0 + gate_in * (1.0 - sig)))).astype(BF16)

    def rows(width):
        return pl.BlockSpec((BLOCK, width), lambda step, place: (step, 0))

    return scalar_call(
        kernel, scalars, (total // BLOCK,),
        (normed, mixed, hidden, upstream, gain_out, *pieces),
        [rows(D), rows(E), rows(D), rows(D), whole((8, E))]
        + [whole((REST, TILE))] * (2 * SEQS),
        [
            jax.ShapeDtypeStruct((total, D), BF16),
            jax.ShapeDtypeStruct((total, E), BF16),
            jax.ShapeDtypeStruct((total, E), BF16),
            jax.ShapeDtypeStruct((total, E), BF16),
            jax.ShapeDtypeStruct((D, total), BF16),
            jax.ShapeDtypeStruct((8, E), F32),
            jax.ShapeDtypeStruct((D, E), BF16),
        ],
        [rows(D), rows(E), rows(E), rows(E), pl.BlockSpec((D, BLOCK), lambda step, place: (0, step)), whole((8, E)),
         whole((D, E))],
        scratch=[pltpu.VMEM((D, E), BF16)],
        name="gated_norm",
        flops=19 * total * D * E,
    )


def input_grad(gate_grad, pre_grad, hidden, upstream, gain_in, inner_weights, small_weights, gate_weights, early):
    total = hidden.shape[0]
    count = len(early)

    def kernel(gate_ref, pre_ref, hidden_ref, upstream_ref, gain_ref, inner_w, small_w, gate_w, *refs):
        early_refs, (out_ref, gain_grad_ref, *sums) = refs[:count], refs[count:]

        @pl.when(pl.program_id(0) == 0)
        def start():
            gain_grad_ref[...] = jnp.zeros_like(gain_grad_ref)

        for core, ref in enumerate(sums):
            ref[...] = sum(early_ref[core].astype(F32) for early_ref in early_refs)
        grad = dot(pre_ref[:, XW:], small_w[...])
        grad = grad + dot_nt(pre_ref[:, :XW], inner_w[...])
        grad = grad + dot_nt(gate_ref[...], gate_w[...])
        value = hidden_ref[...].astype(F32)
        scale = lax.rsqrt(jnp.mean(value * value, -1, keepdims=True) + NORM_EPS)
        unit = value * scale
        gain_grad_ref[0:1] += jnp.sum(grad * unit, 0, keepdims=True)
        pulled = grad * gain_ref[0:1]
        inner = scale * (pulled - unit * jnp.mean(pulled * unit, -1, keepdims=True))
        out_ref[...] = (upstream_ref[...].astype(F32) + inner).astype(BF16)

    steps = total // BLOCK

    def rows(width):
        return pl.BlockSpec((BLOCK, width), lambda step: (step, 0))

    outs = [jax.ShapeDtypeStruct((total, D), BF16), jax.ShapeDtypeStruct((8, D), F32)]
    out_specs = [rows(D), whole((8, D))]
    if early:
        outs += [jax.ShapeDtypeStruct((REST, TILE), F32)] * 2
        out_specs += [pl.BlockSpec((REST // steps, TILE), lambda step: (step, 0))] * 2
    return pl.pallas_call(
        kernel,
        grid=(steps,),
        in_specs=[rows(E), rows(PW), rows(D), rows(D), whole((8, D)), whole((D, XW)), whole((TILE, D)), whole((D, E))]
        + [pl.BlockSpec((2, REST // steps, TILE), lambda step: (0, step, 0))] * count,
        out_specs=out_specs,
        out_shape=outs,
        compiler_params=pltpu.CompilerParams(vmem_limit_bytes=VMEM_BYTES),
        cost_estimate=pl.CostEstimate(flops=1, bytes_accessed=1, transcendentals=0),
        name="input_grad",
    )(gate_grad, pre_grad, hidden, upstream, gain_in, inner_weights, small_weights, gate_weights, *early)


def early_grads(scalars, normed_t, gate_grad, branch_t, gated_low):
    total = normed_t.shape[1]

    def kernel(place, normed_ref, gate_ref, branch_ref, gated_ref, *refs):
        outs, value_ref = refs[:SEQS], refs[SEQS]
        step = pl.program_id(0)

        @pl.when(step < 2)
        def gates():
            value_ref[...] = dot(normed_ref[...], gate_ref[...]).astype(BF16)
            rows = pl.ds(pl.multiple_of((step ^ (place[1] & 1)) * ROWS_ZX, ROWS_ZX), ROWS_ZX)
            for index in range(SEQS):
                source = seq_rows(place, index, ROWS_ZX)
                for core in range(2):
                    outs[index][core ^ place[2], rows, :] = value_ref[source, core * TILE : (core + 1) * TILE]

        @pl.when(step >= 2)
        def weights():
            value_ref[...] = dot(branch_ref[...], gated_ref[...]).astype(BF16)
            for index in range(SEQS):
                seq = place[0] ^ index

                @pl.when(seq // 2 == step - 2)
                def store():
                    cols = pl.ds(pl.multiple_of((seq % 2) * TILE, QB), TILE)
                    for tok in range(8):
                        row = 2 * ROWS_ZX + ((tok >> 1) ^ place[1]) * ROWS_OUT
                        rows = pl.ds(pl.multiple_of(row, ROWS_OUT), ROWS_OUT)
                        outs[index][(tok & 1) ^ place[2], rows, :] = value_ref[
                            tok * ROWS_OUT : (tok + 1) * ROWS_OUT, cols
                        ]

    shape = (2, 2 * ROWS_ZX + CHIPS * ROWS_OUT, TILE)
    return scalar_call(
        kernel, scalars, (4,), (normed_t, gate_grad, branch_t, gated_low),
        [
            whole((D, total)),
            pl.BlockSpec((total, 2 * TILE), lambda step, place: (0, jnp.minimum(step, 1))),
            whole((D, total)),
            pl.BlockSpec((total, 2 * TILE), lambda step, place: (0, jnp.maximum(step - 2, 0))),
        ],
        [jax.ShapeDtypeStruct(shape, BF16)] * SEQS,
        [whole(shape)] * SEQS,
        scratch=[pltpu.VMEM((D, 2 * TILE), BF16)],
        name="early_grads",
    )


def small_gradients(taps_ref, gain_in_ref, gain_out_ref, ssm_ref, out_ref):
    out_ref[...] = jnp.zeros_like(out_ref)
    line = 0
    for ref, source in [(taps_ref, tap) for tap in range(K)] + [
        (gain_in_ref, 0), (gain_out_ref, 0), (taps_ref, K), (ssm_ref, 2),
    ]:
        for base in range(0, ref.shape[1], QB):
            row, col = line // 3, line % 3 * QB
            out_ref[row : row + 1, col : col + QB] = ref[source : source + 1, base : base + QB]
            line += 1


def late_grads(scalars, normed_t, pre_grad, sibling_t, sibling_grad, smalls):
    total = normed_t.shape[1]
    steps = total // BLOCK
    row_map, col_map = small_maps()

    def kernel(
        place, own_t_ref, other_t_ref, grad_ref, other_ref, row_ref, col_ref, taps_ref, gain_in_ref, gain_out_ref, ssm_ref,
        *refs,
    ):
        outs, (vector_ref, wide_sum, small_sum, small_value) = refs[:SEQS], refs[SEQS:]
        step = pl.program_id(0)

        @pl.when(step == 0)
        def start():
            wide_sum[...] = jnp.zeros_like(wide_sum)
            small_sum[...] = jnp.zeros_like(small_sum)

        both_t = jnp.concatenate([own_t_ref[...], other_t_ref[...]], 1)
        tiles = []
        for chip in range(2):
            col = pl.multiple_of((2 * chip + place[2]) * TILE, QB)
            tile = [grad_ref[:, pl.ds(col, TILE)], other_ref[:, chip * TILE : (chip + 1) * TILE]]
            tiles.append(jnp.concatenate(tile, 0))
        wide_sum[...] += dot(both_t, jnp.concatenate(tiles, 1))
        small = jnp.concatenate([grad_ref[:, XW:], other_ref[:, 2 * TILE :]], 0)
        small_sum[...] += dot_nt(small.T, both_t)

        @pl.when(step == steps - 1)
        def finish():
            small_gradients(taps_ref, gain_in_ref, gain_out_ref, ssm_ref, vector_ref)
            result = jnp.zeros((8 * ROWS_BC, SEQS * BC_LANES), F32)
            for part in split(small_sum[...]):
                result = result + dot_nt(dot_tn(row_ref[...], part).astype(BF16), col_ref[...])
            small_value[...] = result
            line = iota((ROWS_BC, TILE), 0)
            rest = jnp.zeros((ROWS_BC, TILE - BC_LANES), F32)
            for index in range(SEQS):
                source = seq_rows(place, index, ROWS_ZX)
                for chip in range(2):
                    cols = pl.ds(pl.multiple_of((chip ^ (place[1] & 1)) * TILE, QB), TILE)
                    outs[index][chip * ROWS_ZX : (chip + 1) * ROWS_ZX, :] = wide_sum[source, cols].astype(BF16)
                cols = pl.ds(pl.multiple_of((place[0] ^ index) * BC_LANES, BC_LANES), BC_LANES)
                for pair in range(CHIPS // 2):
                    value = jnp.zeros((ROWS_BC, TILE), F32)
                    chunks = []
                    for chip in (2 * pair, 2 * pair + 1):
                        tok = 2 * (chip ^ place[1]) + place[2]
                        rows = pl.ds(pl.multiple_of(tok * ROWS_BC, ROWS_BC), ROWS_BC)
                        value = value + half_row(jnp.concatenate([small_value[rows, cols], rest], 1), chip)
                        for core in range(2):
                            device = (place[0] ^ index) * 8 + (tok ^ core)
                            chunks.extend(split(vector_ref[pl.ds(device, 1), :]))
                    for number, chunk in enumerate(chunks):
                        value = jnp.where(line == CHUNK_ROW + number, chunk.astype(F32), value)
                    outs[index][small_rows(2 * pair), :] = value.astype(BF16)

    piece = jax.ShapeDtypeStruct((PIECE, TILE), BF16)
    columns = pl.BlockSpec((D, BLOCK), lambda step, place: (0, step))

    def rows(width):
        return pl.BlockSpec((BLOCK, width), lambda step, place: (step, 0))

    return scalar_call(
        kernel, scalars, (steps,), (normed_t, sibling_t, pre_grad, sibling_grad, row_map, col_map, *smalls),
        [columns, columns, rows(PW), rows(3 * TILE), whole(row_map.shape), whole(col_map.shape)]
        + [whole(value.shape) for value in smalls],
        [piece] * SEQS,
        [whole(piece.shape)] * SEQS,
        scratch=[
            pltpu.VMEM((8 * SEQS, TILE), F32),
            pltpu.VMEM((D, 2 * TILE), F32),
            pltpu.VMEM((TILE, D), F32),
            pltpu.VMEM((8 * ROWS_BC, SEQS * BC_LANES), F32),
        ],
        name="late_grads",
    )


def whole_call(kernel, inputs, outs, name):
    return pl.pallas_call(
        kernel,
        grid=(1,),
        in_specs=[whole(value.shape) for value in inputs],
        out_specs=[whole(out.shape) for out in outs],
        out_shape=outs,
        compiler_params=pltpu.CompilerParams(vmem_limit_bytes=VMEM_BYTES),
        name=name,
    )(*inputs)


def matrices_step(parts, starts, zx, bc, out, devices):
    (rows_bc_t, cols_bc_t), (rows_out_t, cols_out_t) = bc[0].shape, out[0].shape
    count = len(parts)

    def kernel(*refs):
        part_refs, states, outs = refs[:count], refs[count : count + 9], refs[count + 9 :]

        def total(start, rows):
            return sum(ref[start : start + rows, :].astype(F32) for ref in part_refs)

        small = total(starts[1], starts[2] - starts[1])
        grads = (
            total(0, zx[0].shape[0]),
            small[:rows_bc_t, :cols_bc_t],
            total(starts[2], rows_out_t)[:, :cols_out_t],
        )
        lane = iota((1, QB), 1)
        row = jnp.zeros((1, QB), F32)
        for index, grad in enumerate(grads):
            param, first, second = (ref[...] for ref in states[3 * index : 3 * index + 3])
            first_new, second_new, direction = adam_step(param, grad, first, second)
            outs[3 * index][...] = first_new
            outs[3 * index + 1][...] = second_new
            outs[3 * index + 2][...] = direction
            for slot, value in ((index, param), (3 + index, direction)):
                square = jnp.sum(jnp.sum(value * value, 1, keepdims=True), 0, keepdims=True)
                row = jnp.where(lane == slot, square, row)
        chunks = [jnp.zeros((1, TILE), F32)] * 2
        if small.shape[0] > CHUNK_ROW:
            chunks = [small[first : first + 1] + small[first + 1 : first + 2] for first in (CHUNK_ROW, CHUNK_ROW + 2)]
        outs[9][...] = jnp.broadcast_to(jnp.concatenate([row, *chunks], 1)[None], (devices, 1, QB + 2 * TILE))

    arrays = [*zx, *bc, *out]
    outs = [jax.ShapeDtypeStruct(value.shape, F32) for value in arrays]
    outs.append(jax.ShapeDtypeStruct((devices, 1, QB + 2 * TILE), F32))
    return whole_call(kernel, [*parts, *arrays], outs, "matrices_step")


def pack_rows(parts):
    rows = [0]
    for part in parts:
        rows.append(rows[-1] + part.shape[0])

    def kernel(*refs):
        for index, ref in enumerate(refs[:-1]):
            refs[-1][rows[index] : rows[index + 1], :] = ref[...]

    return whole_call(kernel, parts, [jax.ShapeDtypeStruct((rows[-1], TILE), BF16)], "pack_rows")[0]


def chip_pieces(scalars, late, rest, rest_arrived):
    def kernel(place, *refs):
        late_refs, (own_ref, other_ref), outs = refs[:SEQS], refs[SEQS : SEQS + 2], refs[SEQS + 2 :]
        low = place[1] < 2
        line = iota((ROWS_BC, TILE), 0)
        for index in range(CHIPS):
            rows = slice(index % 2 * ROWS_ZX, (index % 2 + 1) * ROWS_ZX)
            inner = sum(ref[rows, :].astype(F32) for ref in late_refs)
            gates = own_ref[rows, :] + other_ref[rows, :]
            inner, gates = (inner, gates) if index >= 2 else (gates, inner)
            outs[index][:ROWS_ZX, :] = jnp.where(low, inner, gates).astype(BF16)
            both = sum(ref[small_rows(index), :].astype(F32) for ref in late_refs)
            small = half_row(both, index)
            for core in range(2):
                source, first = CHUNK_ROW + 4 * (index % 2) + 2 * core, CHUNK_ROW + 2 * core
                chunk = both[source : source + 1] + both[source + 1 : source + 2]
                rest = chunk - chunk.astype(BF16).astype(F32)
                small = jnp.where(line == first, chunk, jnp.where(line == first + 1, rest, small))
            outs[index][ROWS_ZX : ROWS_ZX + ROWS_BC, :] = small.astype(BF16)
            rows = slice(2 * ROWS_ZX + index * ROWS_OUT, 2 * ROWS_ZX + (index + 1) * ROWS_OUT)
            outs[index][ROWS_ZX + ROWS_BC :, :] = (own_ref[rows, :] + other_ref[rows, :]).astype(BF16)

    shape = (ROWS_ZX + ROWS_BC + ROWS_OUT, TILE)
    return scalar_call(
        kernel, scalars, (1,), (*late, rest, rest_arrived),
        [whole(value.shape) for value in (*late, rest, rest_arrived)],
        [jax.ShapeDtypeStruct(shape, BF16)] * CHIPS,
        [whole(shape)] * CHIPS,
        name="chip_pieces",
    )


def settle(value, name):
    rows = value.shape[1]

    def kernel(value_ref, out_ref):
        out_ref[...] = value_ref[...]

    return pl.pallas_call(
        kernel,
        grid=(value.shape[0] // 2,),
        in_specs=[pl.BlockSpec((2, rows, D), lambda step: (step, 0, 0))],
        out_specs=pl.BlockSpec((2, rows, D), lambda step: (step, 0, 0)),
        out_shape=jax.ShapeDtypeStruct(value.shape, value.dtype),
        name=name,
    )(value)


def last_step(squares, gathered, params, directions, conv, vec):
    def kernel(squares_ref, gathered_ref, *refs):
        conv_refs, vec_refs, refs = refs[6:9], refs[9:12], refs[:6] + refs[12:]
        outs = refs[9:]
        total = jnp.sum(squares_ref[:, :, :QB], 0)
        for index in range(3):
            ratio = jnp.sqrt(total[:, index : index + 1]) / jnp.sqrt(total[:, 3 + index : 4 + index] + UPDATE_EPS)
            refs[6 + index][...] = refs[index][...] - LEARN_RATE * ratio * refs[3 + index][...]
        lines = []
        for line in range(SMALL_ROWS):
            device, base = line // 3, (line % 3 + 1) * QB
            own = gathered_ref[device, :, base : base + QB]
            lines.append(own + gathered_ref[device ^ 1, :, TILE + base : TILE + base + QB])
        grad = jnp.concatenate(lines, 0)

        def rows_of(conv_ref, vec_ref):
            lines = [conv_ref[tap : tap + 1, base : base + QB] for tap in range(K) for base in range(0, CW, QB)]
            return jnp.concatenate([*lines, vec_ref[...]], 0)

        value, first, second = (rows_of(conv_refs[index], vec_refs[index]) for index in range(3))
        first_new, second_new, direction = adam_step(value, grad, first, second)
        where = iota(value.shape, 0) * QB + iota(value.shape, 1)
        lane = iota((1, 8), 1)
        rows = [jnp.concatenate([total[:, 3 * row : 3 * row + 3], jnp.zeros((1, 5), F32)], 1) for row in range(2)]
        spread_ratio = jnp.zeros(value.shape, F32)
        for index in range(5):
            inside = (where >= SMALL_EDGES[index]) & (where < SMALL_EDGES[index + 1])
            sums = []
            for slot, term in enumerate((value, direction)):
                square = jnp.where(inside, term * term, 0.0)
                sums.append(jnp.sum(jnp.sum(square, 1, keepdims=True), 0, keepdims=True))
                rows[slot] = jnp.where(lane == 3 + index, sums[slot], rows[slot])
            ratio = jnp.sqrt(sums[0]) / jnp.sqrt(sums[1] + UPDATE_EPS)
            spread_ratio = jnp.where(inside, ratio, spread_ratio)
        new = value - LEARN_RATE * spread_ratio * direction
        for index, result in enumerate((first_new, second_new, new)):
            for line in range(CONV_ROWS):
                tap, base = line // (CW // QB), line % (CW // QB) * QB
                outs[index][tap : tap + 1, base : base + QB] = result[line : line + 1]
            outs[3 + index][...] = result[CONV_ROWS:]
        outs[6][...] = jnp.sqrt(jnp.concatenate(rows, 0))

    outs = [jax.ShapeDtypeStruct(value.shape, F32) for value in (*params, *conv, *vec)]
    return whole_call(
        kernel, [squares, gathered, *params, *directions, *conv, *vec], outs + [jax.ShapeDtypeStruct((2, 8), F32)],
        "last_step",
    )


def adam_step(param, grad, first, second):
    first_new = FIRST_DECAY * first + (1.0 - FIRST_DECAY) * grad
    second_new = SECOND_DECAY * second + (1.0 - SECOND_DECAY) * grad * grad
    corrected = first_new / (1.0 - FIRST_DECAY**STEP)
    scaled = jnp.sqrt(second_new / (1.0 - SECOND_DECAY**STEP))
    return (first_new, second_new, corrected / (scaled + ADAM_EPS) + WEIGHT_DECAY * param)


def pad_row(values, width):
    return jnp.pad(values, (0, width - values.shape[0]))[None]


def eight_rows(values):
    return jnp.pad(values[None], ((0, 7), (0, 0)))


def hop(value, axis, distance):
    count = lax.axis_size(axis)
    return lax.ppermute(value, axis, [(index, index ^ distance) for index in range(count)])


def chip_groups():
    count = lax.axis_size("tok")
    return [list(range(core, count, 2)) for core in range(2)]


def pair_groups():
    count = lax.axis_size("tok")
    return [[first, first + 1] for first in range(0, count, 2)]


def gather_whole(piece):
    along = lax.all_gather(piece, "tok", axis_index_groups=chip_groups())
    across = lax.all_gather(along, "seq")
    pieces = lax.all_gather(across, "tok", axis_index_groups=pair_groups())
    core, seq, chip, rows, cols = pieces.shape
    return pieces.transpose(1, 3, 2, 0, 4).reshape(seq * rows, chip * core * cols)


def sum_cores(pieces):
    core = lax.axis_index("tok") % 2
    other = lax.dynamic_index_in_dim(pieces, 1 - core, 0, keepdims=False)
    own = lax.dynamic_index_in_dim(pieces, core, 0, keepdims=False)
    return own + hop(other, "tok", 1)


def sum_seq(pieces):
    moved = lax.all_to_all(pieces.astype(BF16), "seq", split_axis=0, concat_axis=0, tiled=True)
    return jnp.sum(moved.astype(F32), 0)


def sum_chips(pieces):
    moved = lax.all_to_all(
        pieces.astype(BF16), "tok", split_axis=0, concat_axis=0, axis_index_groups=chip_groups(), tiled=True
    )
    return jnp.sum(moved.astype(F32), 0)


class AnySlice:
    def __init__(self, w_zx, w_bc, w_out, length):
        self.seqs, self.toks = lax.axis_size("seq"), lax.axis_size("tok")
        zero = jnp.zeros((), jnp.int32)
        self.scalars = jnp.stack([zero, zero, zero, length])

    def begin(self, hidden_in, w_zx, w_bc, w_out):
        zx = gather_whole(w_zx.astype(BF16)).reshape(SEQS, ROWS_ZX, 2, 2, 2, TILE).transpose(2, 4, 0, 3, 1, 5)
        zx = zx.reshape(2, 2 * SEQS, 2 * ROWS_ZX, TILE)
        small = gather_whole(w_bc.astype(BF16)).reshape(SEQS, ROWS_ZX, CHIPS, 2, BC_EACH).transpose(3, 0, 2, 4, 1)
        small = jnp.pad(small, ((0, 0),) * 3 + ((0, ROWS_BC - BC_EACH), (0, 0)))
        small = small.reshape(2 * SEQS, CHIPS // 2, 2, ROWS_BC, ROWS_ZX).transpose(0, 1, 3, 2, 4)
        small = small.reshape(2 * SEQS, CHIPS // 2 * ROWS_BC, TILE)
        out = gather_whole(w_out.astype(BF16)).reshape(SEQS, TILE, CHIPS, 2, ROWS_OUT).transpose(3, 0, 2, 4, 1)
        self.rest = tuple(jnp.concatenate([zx[0], out.reshape(2 * SEQS, CHIPS * ROWS_OUT, TILE)], 1))
        return hidden_in, tuple(jnp.concatenate([zx[1], small], 1))

    def before_forward(self, *values):
        return values

    def after_forward(self, *values):
        return (*values, self.rest)

    def before_backward(self, normed, normed_t, gate_grad, branch_t, gated_low, *values):
        self.gate_grad = dot_tn(normed, gate_grad)
        self.out_grad = dot(branch_t, gated_low).T
        return values

    def after_backward(self, *values):
        return values

    def cut(self, array):
        rows, cols = array.shape
        shape = (self.seqs, rows // self.seqs, self.toks // 2, 2, cols // self.toks)
        return array.reshape(shape).transpose(3, 0, 2, 1, 4)

    def finish(self, normed, normed_t, pre_grad, other_grad, back, send, hidden_out, smalls):
        hidden_grad, gain_in_grad = back(pre_grad, ())
        columns = jnp.concatenate([self.gate_grad, dot_tn(normed, pre_grad[:, :XW])], 1)
        small = dot_tn(normed, pre_grad[:, XW:])[:, :BC_COLS]
        columns, small, out = (sum_chips(sum_seq(sum_cores(self.cut(value)))) for value in (columns, small, self.out_grad))
        width = columns.shape[1]
        small, out = (jnp.pad(value.T, ((0, 0), (0, width - value.shape[0]))) for value in (small, out))
        taps_grad, gain_out_grad, ssm_grad = smalls
        vector = jnp.concatenate(
            [taps_grad[:K].reshape(-1), gain_in_grad[0], gain_out_grad[0], taps_grad[K], ssm_grad[2]]
        )
        for axis in ("tok", "seq"):
            distance = 1
            while distance < lax.axis_size(axis):
                vector = vector + hop(vector, axis, distance)
                distance *= 2
        vector = jnp.pad(vector, (0, SMALL_ROWS * QB - vector.shape[0])).reshape(-1, 1, TILE)
        self.vector = jnp.pad(vector, ((0, 0), (0, 0), (QB, TILE)))
        self.starts = (0, columns.shape[0], columns.shape[0] + small.shape[0])
        return (jnp.concatenate([columns, small, out], 0),), send(hidden_grad), hidden_out

    def chunks(self, gathered):
        return self.vector


class ThisSlice:
    def __init__(self, w_zx, w_bc, w_out, length):
        tok = lax.axis_index("tok")
        self.low = tok < 4
        self.scalars = jnp.stack([lax.axis_index("seq"), tok // 2, tok % 2, length]).astype(jnp.int32)

    def chips(self, value):
        return [value] + [hop(value, "tok", 2 * distance) for distance in range(1, CHIPS)]

    def seqs(self, value):
        return [value] + [hop(value, "seq", distance) for distance in range(1, SEQS)]

    def others(self, values):
        return [hop(value, "tok", 1) for value in values]

    def begin(self, hidden_in, w_zx, w_bc, w_out):
        small = jnp.pad(w_bc.astype(BF16).T, ((0, ROWS_BC - BC_EACH), (0, TILE - ROWS_ZX)))
        first = self.chips(jnp.concatenate([w_zx.astype(BF16), small], 0))
        inner = [jnp.where(self.low, first[2 + index], first[index])[:ROWS_ZX] for index in range(2)]
        halves_of = [value[ROWS_ZX : ROWS_ZX + ROWS_BC, :ROWS_ZX] for value in first]
        small = [jnp.concatenate(halves_of[index : index + 2], 1) for index in range(0, CHIPS, 2)]
        inner = jnp.concatenate(inner + small, 0)
        hidden_in, inner, first = lax.optimization_barrier((hidden_in, inner, first))
        inner = self.seqs(inner)
        inner, first, w_out = lax.optimization_barrier((inner, first, w_out))
        self.gate = [jnp.where(self.low, first[index], first[2 + index])[:ROWS_ZX] for index in range(2)]
        self.out = self.chips(w_out.astype(BF16).T)
        return hidden_in, inner + self.others(inner)

    def before_forward(self, *values):
        *values, out = lax.optimization_barrier((*values, self.out))
        self.rest = self.seqs(pack_rows(self.gate + out))
        return values

    def after_forward(self, *values):
        *values, rest = lax.optimization_barrier((*values, self.rest))
        return (*values, rest + self.others(rest))

    def before_backward(self, normed, normed_t, gate_grad, branch_t, gated_low, *values):
        early = early_grads(self.scalars, normed_t, gate_grad, branch_t, gated_low)
        early, values, normed_t = lax.optimization_barrier((tuple(early), values, normed_t))
        self.early = (early[0],) + tuple(hop(early[index], "seq", index) for index in range(1, SEQS))
        self.sibling_t = hop(normed_t, "tok", 1)
        return values

    def after_backward(self, *values):
        values, self.early, self.sibling_t = lax.optimization_barrier((values, self.early, self.sibling_t))
        return values

    def total(self, parts):
        return sum(part.astype(F32) for part in parts)

    def by_seq(self, pieces):
        return [pieces[0]] + [hop(pieces[index], "seq", index) for index in range(1, SEQS)]

    def by_chips(self, pieces):
        return [pieces[0]] + [hop(pieces[index], "tok", 2 * index) for index in range(1, CHIPS)]

    def tree(self, parts):
        return (parts[0] + parts[1]) + (parts[2] + parts[3])

    def finish(self, normed, normed_t, pre_grad, other_grad, back, send, hidden_out, smalls):
        sibling_grad = hop(other_grad, "tok", 1)
        hidden_grad, gain_in_grad, rest, other_rest = back(pre_grad, self.early)
        hidden_grad, rest, other_rest, pre_grad, sibling_grad = lax.optimization_barrier(
            (hidden_grad, rest, other_rest, pre_grad, sibling_grad)
        )
        hidden_grad = send(hidden_grad)
        taps_grad, gain_out_grad, ssm_grad = smalls
        rest_arrived = hop(other_rest, "tok", 1)
        late = late_grads(
            self.scalars, normed_t, pre_grad, self.sibling_t, sibling_grad,
            (taps_grad, gain_in_grad, gain_out_grad, ssm_grad),
        )

        late, hidden_out, rest, rest_arrived = lax.optimization_barrier((late, hidden_out, rest, rest_arrived))
        late = self.by_seq(late)
        hidden_out = settle(hidden_out, "settle_out")
        late, hidden_out = lax.optimization_barrier((late, hidden_out))
        joint = chip_pieces(self.scalars, late, rest, rest_arrived)

        joint, hidden_grad = lax.optimization_barrier((joint, hidden_grad))
        hidden_grad = settle(hidden_grad, "settle_grad")
        joint = self.by_chips(joint)
        joint, hidden_grad = lax.optimization_barrier((joint, hidden_grad))
        self.starts = (0, ROWS_ZX, ROWS_ZX + ROWS_BC)
        return joint, hidden_grad, hidden_out

    def chunks(self, gathered):
        return gathered


def per_device(
    hidden_in, out_grad, lengths, w_zx, m_zx, v_zx, w_bc, m_bc, v_bc, w_out, m_out, v_out,
    conv_w, m_conv, v_conv, vectors, m_vec, v_vec,
):
    toks = lax.axis_size("tok")
    seq_group, local_len, _ = hidden_in.shape
    assert seq_group == toks
    total = seq_group * local_len

    def to_sequence(value):
        return lax.all_to_all(value, "tok", split_axis=0, concat_axis=0, tiled=True).reshape(total, D)

    def to_positions(value):
        return lax.all_to_all(
            value.reshape(seq_group, local_len, D), "tok", split_axis=0, concat_axis=0, tiled=True
        )

    length = lax.dynamic_index_in_dim(lengths, lax.axis_index("tok"), 0, keepdims=False)
    weights = (ThisSlice if (lax.axis_size("seq"), toks) == (4, 8) else AnySlice)(w_zx, w_bc, w_out, length)
    hidden_in, pieces = weights.begin(hidden_in, w_zx, w_bc, w_out)
    hidden = to_sequence(hidden_in)

    gain_in = eight_rows(vectors[:D])
    gain_out = eight_rows(vectors[D : D + E])
    conv_bias = vectors[D + E : D + E + CW]
    ssm_params = vectors[D + E + CW :]
    delta_bias, decay_log, skip_gain = ssm_params[: 2 * H], ssm_params[2 * H : 4 * H], ssm_params[4 * H :]
    taps = jnp.pad(jnp.concatenate([conv_w, conv_bias[None]], 0), ((0, 3), (0, 0)))
    ssm = jnp.pad(jnp.concatenate([pad_row(delta_bias, QB), pad_row(jnp.exp(decay_log), QB)], 0), ((0, 6), (0, 0)))
    skip = eight_rows(jnp.repeat(skip_gain, P_SIZE))

    inner_weights, small_weights = join_weights(weights.scalars, pieces)
    normed, normed_t, pre = project(hidden, gain_in, inner_weights, small_weights)
    pre, out_grad = weights.before_forward(pre, out_grad)
    upstream = to_sequence(out_grad)
    conv_low, mixed, run, delta, ahead, behind, slope = scan_forward(weights.scalars, pre, taps, ssm, skip)
    mixed, upstream, rest = weights.after_forward(mixed, upstream)

    hidden_out, gated_low, mixed_grad, gate_grad, branch_t, gain_out_grad, gate_weights = gated_norm(
        weights.scalars, normed, mixed, hidden, upstream, gain_out, rest
    )
    mixed_grad, hidden_out = weights.before_backward(
        normed, normed_t, gate_grad, branch_t, gated_low, mixed_grad, hidden_out
    )
    hidden_out = to_positions(hidden_out)

    pre_grad, other_grad, taps_grad, ssm_grad, skip_grad = scan_backward(
        weights.scalars, mixed_grad, conv_low, pre, slope, run, delta, ahead, behind, taps, ssm, skip
    )
    pre_grad, other_grad, hidden_out = weights.after_backward(pre_grad, other_grad, hidden_out)

    def back(pre_grad, early):
        return input_grad(
            gate_grad, pre_grad, hidden, upstream, gain_in, inner_weights, small_weights, gate_weights, early
        )

    parts, hidden_grad, hidden_out = weights.finish(
        normed, normed_t, pre_grad, other_grad, back, to_positions, hidden_out, (taps_grad, gain_out_grad, ssm_grad)
    )
    devices = lax.axis_size("seq") * toks
    w_bc_t, w_out_t = w_bc.T, w_out.T
    *stepped, squares = matrices_step(
        parts, weights.starts, (w_zx, m_zx, v_zx), (w_bc_t, m_bc.T, v_bc.T), (w_out_t, m_out.T, v_out.T), devices
    )
    squares = lax.all_to_all(squares, ("seq", "tok"), split_axis=0, concat_axis=0, tiled=True)

    def vector_rows(vector):
        return jnp.pad(vector, (0, (SMALL_ROWS - CONV_ROWS) * QB - vector.shape[0])).reshape(-1, QB)

    zx_new, bc_new, out_new, conv_first, conv_second, conv_new, *small_new, norms = last_step(
        squares, weights.chunks(squares), (w_zx, w_bc_t, w_out_t), stepped[2::3], (conv_w, m_conv, v_conv),
        tuple(vector_rows(value) for value in (vectors, m_vec, v_vec)),
    )
    vec_first, vec_second, vectors_new = (value.reshape(-1)[: vectors.shape[0]] for value in small_new)
    return (
        hidden_out,
        hidden_grad,
        stepped[0],
        stepped[1],
        zx_new,
        stepped[3].T,
        stepped[4].T,
        bc_new.T,
        stepped[6].T,
        stepped[7].T,
        out_new.T,
        conv_first,
        conv_second,
        conv_new,
        vec_first,
        vec_second,
        vectors_new,
        norms,
    )


def solution(mesh):
    placed = (
        P("seq", "tok", None),
        P("seq", "tok", None),
        P("seq"),
        P("seq", "tok"),
        P("seq", "tok"),
        P("seq", "tok"),
        P("seq", "tok"),
        P("seq", "tok"),
        P("seq", "tok"),
        P("seq", "tok"),
        P("seq", "tok"),
        P("seq", "tok"),
        P(),
        P(),
        P(),
        P(),
        P(),
        P(),
    )
    return jax.shard_map(
        per_device,
        mesh=mesh,
        in_specs=placed,
        out_specs=(
            P("seq", "tok", None),
            P("seq", "tok", None),
            P("seq", "tok"),
            P("seq", "tok"),
            P("seq", "tok"),
            P("seq", "tok"),
            P("seq", "tok"),
            P("seq", "tok"),
            P("seq", "tok"),
            P("seq", "tok"),
            P("seq", "tok"),
            P(),
            P(),
            P(),
            P(),
            P(),
            P(),
            P(),
        ),
        check_vma=False,
    )
```
